32 devices in a mesh: seq: 16 (over z, y, x), frm: 2 (over core).
Axes of the slice: x: 2, y: 2, z: 4, core: 2. Of those that a mesh axis runs over, the one named last changes fastest.
Arguments:
- hidden: bfloat16 [32, 448, 768], P('seq'), may hold values from -6 to 6
- encoder: bfloat16 [32, 1500, 768], P('seq', 'frm'), may hold values from -6 to 6
- cotangent: bfloat16 [32, 448, 768], P('seq'), may hold values from -6 to 6
- lengths: int32 [32], P('seq'), may hold values from 56 to 448
- frame_counts: int32 [32], P('seq'), may hold values from 187 to 1500
- corpus_ids: int32 [32], P('seq'), may hold values from 0 to 8
- corpus_weights: float32 [9], replicated, may hold values from 0.25 to 4
- first_gain: float32 [768], replicated, may hold values from 0.5 to 1.5
- first_shift: float32 [768], replicated, may hold values from -1.25 to 1.25
- self_query: bfloat16 [768, 768], replicated, may hold values from -0.21875 to 0.21875
- self_query_bias: float32 [768], replicated, may hold values from -3 to 3
- self_key: bfloat16 [768, 768], replicated, may hold values from -0.21875 to 0.21875
- self_value: bfloat16 [768, 768], replicated, may hold values from -0.21875 to 0.21875
- self_value_bias: float32 [768], replicated, may hold values from -3 to 3
- self_out: bfloat16 [768, 768], replicated, may hold values from -1.75 to 1.75
- self_out_bias: float32 [768], replicated, may hold values from -1.75 to 1.75
- second_gain: float32 [768], replicated, may hold values from 0.5 to 1.5
- second_shift: float32 [768], replicated, may hold values from -1.25 to 1.25
- cross_query: bfloat16 [768, 768], replicated, may hold values from -0.21875 to 0.21875
- cross_query_bias: float32 [768], replicated, may hold values from -3 to 3
- cross_key: bfloat16 [768, 768], replicated, may hold values from -0.21875 to 0.21875
- cross_value: bfloat16 [768, 768], replicated, may hold values from -0.21875 to 0.21875
- cross_value_bias: float32 [768], replicated, may hold values from -3 to 3
- cross_out: bfloat16 [768, 768], replicated, may hold values from -2.5 to 2.5
- cross_out_bias: float32 [768], replicated, may hold values from -1.75 to 1.75
- third_gain: float32 [768], replicated, may hold values from 0.5 to 1.5
- third_shift: float32 [768], replicated, may hold values from -1.25 to 1.25
- expand_weight: bfloat16 [768, 3072], replicated, may hold values from -0.21875 to 0.21875
- expand_bias: float32 [3072], replicated, may hold values from -3 to 3
- shrink_weight: bfloat16 [3072, 768], replicated, may hold values from -0.109375 to 0.109375
- shrink_bias: float32 [768], replicated, may hold values from -1.75 to 1.75
Outputs:
- output: bfloat16 [32, 448, 768], P('seq')
- grad_hidden: float32 [32, 448, 768], P('seq')
- grad_encoder: float32 [32, 1500, 768], P('seq', 'frm')
- grad_first_gain: float32 [768], P('seq')
- grad_first_shift: float32 [768], P('seq')
- grad_self_query: float32 [768, 768], P(None, 'seq')
- grad_self_query_bias: float32 [768], P('seq')
- grad_self_key: float32 [768, 768], P(None, 'seq')
- grad_self_value: float32 [768, 768], P(None, 'seq')
- grad_self_value_bias: float32 [768], P('seq')
- grad_self_out: float32 [768, 768], P(None, 'seq')
- grad_self_out_bias: float32 [768], P('seq')
- grad_second_gain: float32 [768], P('seq')
- grad_second_shift: float32 [768], P('seq')
- grad_cross_query: float32 [768, 768], P(None, 'seq')
- grad_cross_query_bias: float32 [768], P('seq')
- grad_cross_key: float32 [768, 768], P(None, 'seq')
- grad_cross_value: float32 [768, 768], P(None, 'seq')
- grad_cross_value_bias: float32 [768], P('seq')
- grad_cross_out: float32 [768, 768], P(None, 'seq')
- grad_cross_out_bias: float32 [768], P('seq')
- grad_third_gain: float32 [768], P('seq')
- grad_third_shift: float32 [768], P('seq')
- grad_expand_weight: float32 [768, 3072], P(None, 'seq')
- grad_expand_bias: float32 [3072], P('seq')
- grad_shrink_weight: float32 [3072, 768], P(None, 'seq')
- grad_shrink_bias: float32 [768], P('seq')
The draws below stay inside these ranges and needn't reach their ends.
All inputs are finite; a program needn't handle non-finite values.
Results may differ from the reference program's by a relative error of at most 0.022.
Values may be sent and summed in bfloat16 or wider, within the bound.
A program may use at most 384 MiB of HBM per device.

```python
import math
import jax
import jax.numpy as jnp
from jax import lax

HEADS = 12
HDIM = 64
D = 768
FF = 3072
SLOTS = 448
FRAMES = 1500
CORPORA = 9
TR_DEV = 2
TRANS = 32


def draw_lengths(key, part):
    key = jax.random.fold_in(key, 11)
    keys = jax.random.split(key, 3)
    values = jax.random.randint(keys[0], (TRANS,), SLOTS // 8, SLOTS + 1)
    first = jax.random.randint(keys[1], (), 0, TRANS)
    second = (first + 1 + jax.random.randint(keys[2], (), 0, TRANS - 1)) % TRANS
    return values.at[first].set(SLOTS).at[second].set(SLOTS // 8).astype(jnp.int32)


def draw_frame_counts(key, part):
    key = jax.random.fold_in(key, 23)
    keys = jax.random.split(key, 5)
    groups = TRANS // TR_DEV
    values = jax.random.randint(keys[0], (groups, TR_DEV), FRAMES // 8, FRAMES + 1)
    chosen = jax.random.randint(keys[1], (groups,), 0, TR_DEV)
    far_counts = jax.random.randint(keys[2], (groups,), 3 * FRAMES // 4 + 1, FRAMES + 1)
    places = jnp.arange(TR_DEV)[None, :] == chosen[:, None]
    values = jnp.where(places, far_counts[:, None], values)
    top_group = jax.random.randint(keys[3], (), 0, groups)
    least_group = jax.random.randint(keys[4], (), 0, groups)
    values = values.at[top_group, chosen[top_group]].set(FRAMES)
    values = values.at[least_group, (chosen[least_group] + 1) % TR_DEV].set(FRAMES // 8)
    return values.reshape(TRANS).astype(jnp.int32)


def place_ends(array, key, smallest, top_value):
    longest = array.shape.index(max(array.shape))
    spots = []
    for shift in (0, 1):
        where = [jax.random.randint(jax.random.fold_in(key, axis), (), 0, length) for axis, length in enumerate(array.shape)]
        where[longest] = (where[longest] + shift) % array.shape[longest]
        spots.append(tuple(where))
    return array.at[spots[0]].set(smallest).at[spots[1]].set(top_value)


def raised(array, stream_key, source, target, blocks, factor):
    def block_of(axis_at):
        return (jnp.arange(array.shape[axis_at]) // (array.shape[axis_at] // blocks)).reshape((-1,) + (1,) * (array.ndim - 1 - axis_at))

    first = jax.random.permutation(stream_key, blocks)[block_of(target)]
    second = (block_of(target) + blocks // 2) % blocks
    return jnp.where((block_of(source) == first) | (block_of(source) == second), factor * array, array)


def levels(stream_key, dims, cuts, smallest, high):
    def one(axis_at, parts):
        heights = jax.random.uniform(jax.random.fold_in(jax.random.fold_in(stream_key, 6), axis_at), (parts,), jnp.float32, smallest / len(cuts), high / len(cuts))
        return jnp.repeat(jnp.exp(heights), dims[axis_at] // parts).reshape((-1,) + (1,) * (len(dims) - axis_at - 1))

    loudness = one(*cuts[0])
    for cut in cuts[1:]:
        loudness = loudness * one(*cut)
    return loudness


def scatter_about(key, extent, scale, most, cuts=(), dtype=jnp.bfloat16):
    drawn = jax.random.normal(key, extent, jnp.float32) * scale
    if len(cuts) > 0:
        drawn = levels(key, extent, cuts, -0.22, 0.18) * drawn
    return jnp.clip(drawn, min=-most, max=most).astype(dtype)


def gaussian_with(stream_key, shape, scale, most, cuts, heavy, kind=jnp.bfloat16):
    drawn = scale * jax.random.normal(stream_key, shape, jnp.float32)
    if cuts:
        drawn = drawn * levels(stream_key, shape, cuts, -0.22, 0.18)
    return jnp.clip(raised(drawn, jax.random.fold_in(stream_key, 3), *heavy), -most, most).astype(kind)


def setup_inputs(seed: int = 0) -> dict:
    key_list = jax.random.split(jax.random.key(seed), 32)
    hidden = scatter_about(key_list[0], (TRANS, SLOTS, D), 1.0, 6.0, ((0, 16),))
    encoder = scatter_about(key_list[1], (TRANS, FRAMES, D), 1.0, 6.0, ((0, 16), (1, 2)))
    cotangent = gaussian_with(key_list[2], (TRANS, SLOTS, D), 1.0, 6.0, ((0, 16),), (0, 2, 16, 2.0))
    lengths = draw_lengths(jax.random.fold_in(key_list[31], 71), 0)
    frame_counts = draw_frame_counts(jax.random.fold_in(key_list[31], 71), 0)
    corpus_ids = place_ends(jax.random.randint(key_list[5], (TRANS,), 0, CORPORA), jax.random.fold_in(key_list[5], 1), 0, CORPORA - 1).astype(jnp.int32)
    corpus_weights = jnp.clip(jnp.exp(jax.random.uniform(key_list[6], (CORPORA,), jnp.float32, math.log(0.25), math.log(4.0))), 0.25, 4.0)
    first_gain = jnp.clip(1.0 + 0.1 * jax.random.normal(key_list[7], (D,), jnp.float32), 0.5, 1.5)
    first_shift = scatter_about(key_list[8], (D,), 0.2, 1.25, (), jnp.float32)
    self_query = scatter_about(key_list[9], (D, D), D ** -0.5, 0.21875)
    self_query_bias = scatter_about(key_list[10], (D,), 0.5, 3.0, (), jnp.float32)
    self_key = scatter_about(key_list[11], (D, D), D ** -0.5, 0.21875)
    self_value = scatter_about(key_list[12], (D, D), D ** -0.5, 0.21875)
    self_value_bias = scatter_about(key_list[13], (D,), 0.5, 3.0, (), jnp.float32)
    self_out = scatter_about(key_list[14], (D, D), (D // 64) ** -0.5, 1.75)
    self_out_bias = scatter_about(key_list[15], (D,), 0.3, 1.75, (), jnp.float32)
    second_gain = jnp.clip(1.0 + 0.1 * jax.random.normal(key_list[16], (D,), jnp.float32), 0.5, 1.5)
    second_shift = scatter_about(key_list[17], (D,), 0.2, 1.25, (), jnp.float32)
    cross_query = scatter_about(key_list[18], (D, D), D ** -0.5, 0.21875)
    cross_query_bias = scatter_about(key_list[19], (D,), 0.5, 3.0, (), jnp.float32)
    cross_key = scatter_about(key_list[20], (D, D), D ** -0.5, 0.21875)
    cross_value = scatter_about(key_list[21], (D, D), D ** -0.5, 0.21875)
    cross_value_bias = scatter_about(key_list[22], (D,), 0.5, 3.0, (), jnp.float32)
    cross_out = scatter_about(key_list[23], (D, D), (D // 128) ** -0.5, 2.5)
    cross_out_bias = scatter_about(key_list[24], (D,), 0.3, 1.75, (), jnp.float32)
    third_gain = jnp.clip(1.0 + 0.1 * jax.random.normal(key_list[25], (D,), jnp.float32), 0.5, 1.5)
    third_shift = scatter_about(key_list[26], (D,), 0.2, 1.25, (), jnp.float32)
    expand_weight = scatter_about(key_list[27], (D, FF), D ** -0.5, 0.21875)
    expand_bias = scatter_about(key_list[28], (FF,), 0.5, 3.0, (), jnp.float32)
    shrink_weight = scatter_about(key_list[29], (FF, D), FF ** -0.5, 0.109375)
    shrink_bias = scatter_about(key_list[30], (D,), 0.3, 1.75, (), jnp.float32)
    return dict(hidden=hidden, encoder=encoder, cotangent=cotangent, lengths=lengths, frame_counts=frame_counts, corpus_ids=corpus_ids, corpus_weights=corpus_weights, first_gain=first_gain, first_shift=first_shift, self_query=self_query, self_query_bias=self_query_bias, self_key=self_key, self_value=self_value, self_value_bias=self_value_bias, self_out=self_out, self_out_bias=self_out_bias, second_gain=second_gain, second_shift=second_shift, cross_query=cross_query, cross_query_bias=cross_query_bias, cross_key=cross_key, cross_value=cross_value, cross_value_bias=cross_value_bias, cross_out=cross_out, cross_out_bias=cross_out_bias, third_gain=third_gain, third_shift=third_shift, expand_weight=expand_weight, expand_bias=expand_bias, shrink_weight=shrink_weight, shrink_bias=shrink_bias)


@jax.custom_vjp
def low(v):
    return lax.optimization_barrier(v.astype(jnp.bfloat16)).astype(jnp.float32)

@jax.custom_vjp
def low_back(v):
    return v

def low_keep(v):
    return (low(v), None)

def low_pass(kept, grad):
    return (grad,)

def back_keep(v):
    return (v, None)

def back_low(kept, grad):
    return (low(grad),)
low.defvjp(low_keep, low_pass)
low_back.defvjp(back_keep, back_low)

def project(inputs, weight):
    return jnp.einsum('tld,de->tle', inputs, weight, precision=lax.Precision.HIGHEST)

def layer_norm(value, gain, shift):
    center = lax.optimization_barrier(jnp.mean(value, axis=-1, keepdims=True))
    centered = value - center
    spread = lax.optimization_barrier(jnp.mean(centered * centered, axis=-1, keepdims=True))
    return centered * lax.rsqrt(spread + 1e-05) * gain + shift

def split_heads(value):
    return value.reshape(value.shape[0], value.shape[1], HEADS, HDIM)

def attention(queries, key_rows, value_rows, key_mask):
    scores = low_back(jnp.einsum('tqhd,tkhd->thqk', split_heads(queries), split_heads(key_rows), precision=lax.Precision.HIGHEST))
    scores = jnp.where(key_mask, scores, -1e+30)
    row_top = lax.optimization_barrier(jnp.max(scores, axis=-1, keepdims=True))
    weights = jnp.exp(scores - row_top)
    probs = low(weights / lax.optimization_barrier(jnp.sum(weights, axis=-1, keepdims=True)))
    mixture = jnp.einsum('thqk,tkhd->tqhd', probs, split_heads(value_rows), precision=lax.Precision.HIGHEST)
    return low(low_back(mixture.reshape(queries.shape)))

def decoder_block(params, hidden_rows, encoder_rows, lengths, frame_counts):
    first_gain, first_shift, self_query, self_query_bias, self_key, self_value, self_value_bias, self_out, self_out_bias, second_gain, second_shift, cross_query, cross_query_bias, cross_key, cross_value, cross_value_bias, cross_out, cross_out_bias, third_gain, third_shift, expand_weight, expand_bias, shrink_weight, shrink_bias = params
    scale = HDIM ** (-0.5)
    slot_index = jnp.arange(hidden_rows.shape[1])
    self_mask = (slot_index[None, :, None] >= slot_index[None, None, :]) & (slot_index[None, None, :] < lengths[:, None, None])
    frame_index = jnp.arange(encoder_rows.shape[1])
    cross_mask = (frame_index[None, :] < frame_counts[:, None])[:, None, None, :]
    normed_one = low(layer_norm(hidden_rows, first_gain, first_shift))
    queries = low(low_back((project(normed_one, self_query) + self_query_bias) * scale))
    key_rows = low(low_back(project(normed_one, self_key)))
    value_rows = low(low_back(project(normed_one, self_value) + self_value_bias))
    mixture = attention(queries, key_rows, value_rows, self_mask[:, None])
    after_self = hidden_rows + low_back(project(mixture, self_out) + self_out_bias)
    normed_two = low(layer_norm(after_self, second_gain, second_shift))
    cross_queries = low(low_back((project(normed_two, cross_query) + cross_query_bias) * scale))
    cross_keys = low(low_back(project(encoder_rows, cross_key)))
    cross_values = low(low_back(project(encoder_rows, cross_value) + cross_value_bias))
    cross_mixture = attention(cross_queries, cross_keys, cross_values, cross_mask)
    after_cross = after_self + low_back(project(cross_mixture, cross_out) + cross_out_bias)
    normed_three = low(layer_norm(after_cross, third_gain, third_shift))
    active = low(low_back(jax.nn.gelu(low_back(project(normed_three, expand_weight) + expand_bias), approximate=False)))
    return after_cross + low_back(project(active, shrink_weight) + shrink_bias)

def reference(hidden, encoder, cotangent, lengths, frame_counts, corpus_ids, corpus_weights, first_gain, first_shift, self_query, self_query_bias, self_key, self_value, self_value_bias, self_out, self_out_bias, second_gain, second_shift, cross_query, cross_query_bias, cross_key, cross_value, cross_value_bias, cross_out, cross_out_bias, third_gain, third_shift, expand_weight, expand_bias, shrink_weight, shrink_bias):
    params = tuple((item.astype(jnp.float32) for item in (first_gain, first_shift, self_query, self_query_bias, self_key, self_value, self_value_bias, self_out, self_out_bias, second_gain, second_shift, cross_query, cross_query_bias, cross_key, cross_value, cross_value_bias, cross_out, cross_out_bias, third_gain, third_shift, expand_weight, expand_bias, shrink_weight, shrink_bias)))
    group_size = 8
    num_trans = hidden.shape[0]

    def regroup(value):
        return value.reshape((num_trans // group_size, group_size) + value.shape[1:])
    saved_block = jax.checkpoint(decoder_block)

    def forward(weights, hidden_rows, encoder_rows):

        def scan_step(unused, pieces):
            return (unused, saved_block(weights, pieces[0], pieces[1], pieces[2], pieces[3]))
        unused, outputs = lax.scan(scan_step, jnp.zeros((), jnp.float32), (regroup(hidden_rows), regroup(encoder_rows), regroup(lengths), regroup(frame_counts)))
        return outputs.reshape(hidden_rows.shape)
    result, pullback = jax.vjp(forward, params, hidden.astype(jnp.float32), encoder.astype(jnp.float32))
    slot_index = jnp.arange(hidden.shape[1])
    row_weight = corpus_weights[corpus_ids][:, None] * (slot_index[None, :] < lengths[:, None]).astype(jnp.float32)
    grad_params, grad_hidden, grad_encoder = pullback(cotangent.astype(jnp.float32) * row_weight[:, :, None])
    return (result.astype(jnp.bfloat16), grad_hidden, grad_encoder) + tuple(grad_params)
```

```python
import jax
import jax.numpy as jnp
from jax import lax
from jax.sharding import PartitionSpec as P

HEADS = 12
HDIM = 64
BF16 = jnp.bfloat16
F32 = jnp.float32


def matmul(left, right):
    return jnp.dot(left, right, preferred_element_type=F32)


def matmul_right_t(left, right):
    return lax.dot_general(left, right, (((1,), (1,)), ((), ())), preferred_element_type=F32)


def matmul_left_t(left, right):
    return lax.dot_general(left, right, (((0,), (0,)), ((), ())), preferred_element_type=F32)


def normalize(value, gain, shift):
    center = jnp.mean(value, axis=-1, keepdims=True)
    centered = value - center
    rstd = lax.rsqrt(jnp.mean(centered * centered, axis=-1, keepdims=True) + 1e-05)
    unit = centered * rstd
    return (unit * gain + shift, unit, rstd)


def normalize_back(grad, unit, rstd, gain):
    scaled = grad * gain
    return rstd * (
        scaled
        - jnp.mean(scaled, axis=-1, keepdims=True)
        - unit * jnp.mean(scaled * unit, axis=-1, keepdims=True)
    )


def heads_view(value):
    return value.reshape(value.shape[0], HEADS, HDIM)


def attention_scores(queries, key_rows, key_mask):
    scores = jnp.einsum("qhd,khd->hqk", queries, key_rows, preferred_element_type=F32)
    return jnp.where(key_mask, scores, -1e30)


def local_softmax(scores):
    row_top = jnp.max(scores, axis=-1, keepdims=True)
    weights = jnp.exp(scores - row_top)
    return weights / jnp.sum(weights, axis=-1, keepdims=True)


def attention_back(probs, dmix, value_rows, queries, key_rows):
    probs_low = probs.astype(BF16)
    dprob = jnp.einsum("qhd,khd->hqk", dmix, value_rows, preferred_element_type=F32)
    inner = jnp.sum(probs * dprob, axis=-1, keepdims=True)
    dscore = (probs * (dprob - inner)).astype(BF16)
    dquery = jnp.einsum("hqk,khd->qhd", dscore, key_rows, preferred_element_type=F32)
    dkeys = jnp.einsum("hqk,qhd->khd", dscore, queries, preferred_element_type=F32)
    dvalues = jnp.einsum("hqk,qhd->khd", probs_low, dmix, preferred_element_type=F32)
    flat = lambda v: v.astype(BF16).reshape(v.shape[0], -1)
    return flat(dquery), flat(dkeys), flat(dvalues)


def exact_gelu(value):
    return jax.nn.gelu(value, approximate=False)


class Links:
    def __init__(self):
        self.chips = lax.axis_size("seq")
        self.halving = self.chips == 16
        self.core = lax.axis_index("frm")
        self.chip = lax.axis_index("seq")

    def move(self, value, where):
        pairs = []
        for chip in range(self.chips):
            for core in range(2):
                to_chip, to_core = where(chip, core)
                pairs.append((chip * 2 + core, to_chip * 2 + to_core))
        return lax.ppermute(value, ("seq", "frm"), pairs)

    def swap(self, value):
        return self.move(value, lambda chip, core: (chip, 1 - core))

    def order(self, core):
        first = 1 + core
        second = 3 - first
        plane = jnp.stack([jnp.int32(0) * core, second, first, jnp.int32(3) + 0 * core])
        plane = plane ^ (self.chip % 4)
        along = jnp.arange(4) ^ (self.chip // 4)
        return (along[None, :] * 4 + plane[:, None]).reshape(16)

    def reduce(self, grads):
        if not self.halving:
            return [
                lax.psum(
                    lax.psum_scatter(g, "seq", scatter_dimension=0, tiled=True).astype(BF16), "frm"
                ).astype(F32)
                for g in grads
            ]
        mine, theirs = [], []
        for g in grads:
            half = g.shape[1] // 2
            cut = g.astype(BF16).reshape(16, g.shape[0] // 16, g.shape[1])
            for core, out in ((self.core, mine), (1 - self.core, theirs)):
                part = lax.dynamic_slice_in_dim(cut, core * half, half, 2)
                out.append(jnp.take(part, self.order(core), axis=0))
        add = lambda a, b: (a.astype(F32) + b.astype(F32)).astype(BF16)
        got = [self.swap(t) for t in theirs]
        keep = [add(m[:8], t[:8]) for m, t in zip(mine, got)]
        send = [add(m[8:], t[8:]) for m, t in zip(mine, got)]
        got = [self.move(s, lambda chip, core: (chip ^ (1 + core), core)) for s in send]
        send = [add(k[4:], t[4:]) for k, t in zip(keep, got)]
        keep = [add(k[:4], t[:4]) for k, t in zip(keep, got)]
        got = [self.move(s, lambda chip, core: (chip ^ (2 - core), core)) for s in send]
        parts = [[add(k[i], t[i]) for i in range(4)] for k, t in zip(keep, got)]
        totals = []
        for p in parts:
            total = p[0].astype(F32)
            for i in (1, 2, 3):
                arrived = self.move(p[i], lambda chip, core, i=i: (chip ^ (4 * i), core))
                total = total + arrived.astype(F32)
            totals.append(total.astype(BF16))
        outs = []
        for total in totals:
            other = self.swap(total)
            first = jnp.where(self.core == 0, total, other)
            second = jnp.where(self.core == 0, other, total)
            outs.append(jnp.concatenate([first, second], axis=1).astype(F32))
        return outs

    def reduce_vectors(self, vectors):
        if not self.halving:
            return [
                lax.psum(
                    lax.psum_scatter(v, "seq", scatter_dimension=0, tiled=True).astype(BF16), "frm"
                ).astype(F32)
                for v in vectors
            ]
        widths = [v.shape[0] // 16 for v in vectors]
        packed = jnp.concatenate([v.reshape(16, -1) for v in vectors], axis=1)
        packed = jnp.pad(packed, ((0, 0), (0, -packed.shape[1] % 1024))).reshape(16, 8, -1)
        packed = jnp.take(packed, self.order(jnp.int32(0)), axis=0)
        packed = packed + self.swap(packed)
        packed = packed[:8] + self.move(packed[8:], lambda chip, core: (chip ^ 1, core))
        packed = packed[:4] + self.move(packed[4:], lambda chip, core: (chip ^ 2, core))
        total = packed[0]
        for i in (1, 2, 3):
            total = total + self.move(packed[i], lambda chip, core, i=i: (chip ^ (4 * i), core))
        total = total.reshape(-1)
        outs, at = [], 0
        for width in widths:
            outs.append(total[at : at + width])
            at += width
        return outs


def shards(
    hidden,
    encoder,
    cotangent,
    lengths,
    frame_counts,
    corpus_ids,
    corpus_weights,
    first_gain,
    first_shift,
    self_query,
    self_query_bias,
    self_key,
    self_value,
    self_value_bias,
    self_out,
    self_out_bias,
    second_gain,
    second_shift,
    cross_query,
    cross_query_bias,
    cross_key,
    cross_value,
    cross_value_bias,
    cross_out,
    cross_out_bias,
    third_gain,
    third_shift,
    expand_weight,
    expand_bias,
    shrink_weight,
    shrink_bias,
):
    links = Links()
    core = links.core
    num_slots, width = hidden.shape[1:]
    local_frames = encoder.shape[1]
    pad_frames = -local_frames % 128
    block = local_frames + pad_frames
    scale = HDIM ** (-0.5)
    scale_low = jnp.asarray(scale, BF16)
    pick = lambda value, index: lax.dynamic_index_in_dim(value, index, 0, keepdims=False)
    length = pick(lengths, core)
    frame_total = pick(frame_counts, core)
    corpus = pick(corpus_ids, core)
    row_scale = jnp.sum(
        jnp.where(jnp.arange(corpus_weights.shape[0]) == corpus, corpus_weights, 0.0)
    )
    own_states = pick(encoder, core)
    far_states = links.swap(pick(encoder, 1 - core))
    padding = ((0, pad_frames), (0, 0))
    states = jnp.concatenate([jnp.pad(own_states, padding), jnp.pad(far_states, padding)])
    place = jnp.arange(2 * block)
    in_half = place % block
    half = jnp.where(place < block, core, 1 - core)
    frame_live = (in_half < local_frames) & (half * local_frames + in_half < frame_total)

    slot_index = jnp.arange(num_slots)
    self_mask = (slot_index[:, None] >= slot_index[None, :]) & (slot_index[None, :] < length)
    inputs = pick(hidden, core).astype(F32)
    normed_one, unit_one, rstd_one = normalize(inputs, first_gain, first_shift)
    low_one = normed_one.astype(BF16)
    queries = heads_view(((matmul(low_one, self_query) + self_query_bias) * scale).astype(BF16))
    key_rows = heads_view(matmul(low_one, self_key).astype(BF16))
    value_rows = heads_view((matmul(low_one, self_value) + self_value_bias).astype(BF16))
    probs = local_softmax(attention_scores(queries, key_rows, self_mask[None]))
    weigh = lambda p, v: jnp.einsum(
        "hqk,khd->qhd", p.astype(BF16), v, preferred_element_type=F32
    ).astype(BF16).reshape(num_slots, width)
    mixture = weigh(probs, value_rows)
    after_self = inputs + matmul(mixture, self_out) + self_out_bias
    normed_two, unit_two, rstd_two = normalize(after_self, second_gain, second_shift)
    low_two = normed_two.astype(BF16)
    cross_queries = heads_view(
        ((matmul(low_two, cross_query) + cross_query_bias) * scale).astype(BF16)
    )
    cross_keys = heads_view(matmul(states, cross_key).astype(BF16))
    cross_values = heads_view((matmul(states, cross_value) + cross_value_bias).astype(BF16))
    cross_probs = local_softmax(
        attention_scores(cross_queries, cross_keys, frame_live[None, None, :])
    )
    cross_mixture = weigh(cross_probs, cross_values)
    after_cross = after_self + matmul(cross_mixture, cross_out) + cross_out_bias
    normed_three, unit_three, rstd_three = normalize(after_cross, third_gain, third_shift)
    low_three = normed_three.astype(BF16)
    pre_active = matmul(low_three, expand_weight) + expand_bias
    active, gelu_back = jax.vjp(exact_gelu, pre_active)
    active_low = active.astype(BF16)
    result = after_cross + matmul(active_low, shrink_weight) + shrink_bias
    output = result.astype(BF16)

    live_rows = (slot_index < length).astype(F32) * row_scale
    grad_result = pick(cotangent, core).astype(F32) * live_rows[:, None]
    dshrink = grad_result.astype(BF16)
    column_sum = lambda v: jnp.sum(v.astype(F32), axis=0)
    dactive = matmul_right_t(dshrink, shrink_weight).astype(BF16)
    dpre = gelu_back(dactive.astype(F32))[0].astype(BF16)
    feed_grads = links.reduce([matmul_left_t(dpre, low_three), matmul_left_t(dshrink, active_low)])
    dnormed_three = matmul_right_t(dpre, expand_weight)
    dafter_cross = grad_result + normalize_back(dnormed_three, unit_three, rstd_three, third_gain)
    dcross = dafter_cross.astype(BF16)
    dcross_mix = heads_view(matmul_right_t(dcross, cross_out).astype(BF16))
    dcq, dck_rows, dcv_rows = attention_back(
        cross_probs, dcross_mix, cross_values, cross_queries, cross_keys
    )
    dcq_scaled = dcq * scale_low
    cross_grads = links.reduce(
        [
            matmul_left_t(dcq_scaled, low_two),
            matmul_left_t(dck_rows, states),
            matmul_left_t(dcv_rows, states),
            matmul_left_t(dcross, cross_mixture),
        ]
    )
    dnormed_two = matmul_right_t(dcq_scaled, cross_query)
    grad_states = matmul_right_t(dck_rows, cross_key) + matmul_right_t(dcv_rows, cross_value)
    dafter_self = dafter_cross + normalize_back(dnormed_two, unit_two, rstd_two, second_gain)
    dself = dafter_self.astype(BF16)
    dself_mix = heads_view(matmul_right_t(dself, self_out).astype(BF16))
    dquery, dkey_rows, dvalue_rows = attention_back(
        probs, dself_mix, value_rows, queries, key_rows
    )
    dquery_scaled = dquery * scale_low
    self_grads = links.reduce(
        [
            matmul_left_t(dquery_scaled, low_one),
            matmul_left_t(dkey_rows, low_one),
            matmul_left_t(dvalue_rows, low_one),
            matmul_left_t(dself, mixture),
        ]
    )
    dnormed_one = (
        matmul_right_t(dquery_scaled, self_query)
        + matmul_right_t(dkey_rows, self_key)
        + matmul_right_t(dvalue_rows, self_value)
    )
    grad_inputs = dafter_self + normalize_back(dnormed_one, unit_one, rstd_one, first_gain)
    vectors = links.reduce_vectors(
        [
            column_sum(dnormed_one * unit_one),
            column_sum(dnormed_one),
            column_sum(dquery_scaled),
            column_sum(dvalue_rows),
            column_sum(dself),
            column_sum(dnormed_two * unit_two),
            column_sum(dnormed_two),
            column_sum(dcq_scaled),
            column_sum(dcv_rows),
            column_sum(dcross),
            column_sum(dnormed_three * unit_three),
            column_sum(dnormed_three),
            column_sum(dpre),
            column_sum(dshrink),
        ]
    )

    def both(own):
        far = links.swap(own)
        return jnp.stack([jnp.where(core == 0, own, far), jnp.where(core == 0, far, own)])

    own_half = grad_states[:local_frames].astype(BF16)
    far_half = links.swap(grad_states[block : block + local_frames].astype(BF16))
    grad_encoder = jnp.stack(
        [jnp.where(core == 0, own_half, far_half), jnp.where(core == 0, far_half, own_half)]
    ).astype(F32)
    t = jnp.transpose
    return (
        both(output),
        both(grad_inputs.astype(BF16)).astype(F32),
        grad_encoder,
        vectors[0],
        vectors[1],
        t(self_grads[0]),
        vectors[2],
        t(self_grads[1]),
        t(self_grads[2]),
        vectors[3],
        t(self_grads[3]),
        vectors[4],
        vectors[5],
        vectors[6],
        t(cross_grads[0]),
        vectors[7],
        t(cross_grads[1]),
        t(cross_grads[2]),
        vectors[8],
        t(cross_grads[3]),
        vectors[9],
        vectors[10],
        vectors[11],
        t(feed_grads[0]),
        vectors[12],
        t(feed_grads[1]),
        vectors[13],
    )


def solution(mesh):
    copied = P()
    return jax.shard_map(
        shards,
        mesh=mesh,
        in_specs=(
            P("seq", None, None),
            P("seq", "frm", None),
            P("seq", None, None),
            P("seq"),
            P("seq"),
            P("seq"),
        )
        + (copied,) * 25,
        out_specs=(P("seq", None, None), P("seq", None, None), P("seq", "frm", None))
        + tuple(
            P(None, "seq") if matrix else P("seq")
            for matrix in (0, 0, 1, 0, 1, 1, 0, 1, 0, 0, 0, 1, 0, 1, 1, 0, 1, 0, 0, 0, 1, 0, 1, 0)
        ),
        check_vma=False,
    )
```

```python
import functools
import jax
import jax.numpy as jnp
from jax import lax
from jax.experimental import pallas as pl
from jax.experimental.pallas import tpu as pltpu
from jax.sharding import PartitionSpec as P

HEADS = 12
HDIM = 64
BF16 = jnp.bfloat16
F32 = jnp.float32
MIB = 1024 * 1024
MESH = pl.DeviceIdType.MESH
VMEM = pl.BlockSpec(memory_space=pltpu.VMEM)
SMEM = pl.BlockSpec(memory_space=pltpu.SMEM)
ANY = pl.BlockSpec(memory_space=pl.ANY)
NEVER = -1e30


def dot(left, right, over=(1, 0)):
    return lax.dot_general(
        left, right, (((over[0],), (over[1],)), ((), ())), preferred_element_type=F32
    )


def shape(*dims, dtype=BF16):
    return jax.ShapeDtypeStruct(dims, dtype)


def unit_of(value):
    center = jnp.mean(value, axis=-1, keepdims=True)
    centered = value - center
    rstd = lax.rsqrt(jnp.mean(centered * centered, axis=-1, keepdims=True) + 1e-05)
    return centered * rstd, rstd


def norm_back(grad, unit, rstd, gain):
    scaled = grad * gain
    return rstd * (
        scaled
        - jnp.mean(scaled, axis=-1, keepdims=True)
        - unit * jnp.mean(scaled * unit, axis=-1, keepdims=True)
    )


def row_blocks(rows, body, step=64):
    def one(i, carry):
        body(pl.ds(pl.multiple_of(i * step, step), step))
        return carry

    lax.fori_loop(0, rows // step, one, 0)


def spread_heads(out, index, flat_t, other):
    for e in range(2):
        lo, hi = (0, HDIM) if e == 0 else (HDIM, 2 * HDIM)
        out[2 * index + e, lo:hi] = flat_t[lo:hi]
        out[2 * index + e, HDIM - lo : 2 * HDIM - lo] = other


def forward_kernel(
    lengths,
    frames,
    hidden,
    g1,
    s1,
    wq,
    bq,
    wk,
    wv,
    bv,
    bo,
    g2,
    s2,
    bcq,
    bcv,
    bco,
    near,
    far,
    wo,
    wcq,
    wck,
    wcv,
    wco,
    h1_out,
    q_out,
    k_out,
    v_out,
    lse1_out,
    mix_out,
    x1_out,
    h2_out,
    cq_out,
    ck_out,
    cv_out,
    lse2_out,
    cmix_out,
    x2_out,
    near_v,
    far_v,
    wo_v,
    wcq_v,
    wck_v,
    wcv_v,
    wco_v,
    h1,
    q,
    k,
    v,
    lse1,
    mix,
    x1,
    h2,
    cq,
    ck,
    cv,
    lse2,
    cmix,
    x2,
    qx,
    bias,
    tail,
    mixed_t,
    scores,
    in_sem,
    out_sem,
    *,
    frames_half,
):
    core = lax.axis_index("frm")
    length = lengths[core]
    frame_total = frames[core]
    loads = {}
    for i, (src, dst) in enumerate(
        ((wo, wo_v), (near, near_v), (far, far_v), (wck, wck_v), (wcv, wcv_v), (wcq, wcq_v), (wco, wco_v))
    ):
        loads[i] = pltpu.make_async_copy(src, dst, in_sem.at[i])
        loads[i].start()
    stores = []

    def store(src, dst):
        copy = pltpu.make_async_copy(src, dst, out_sem.at[len(stores)])
        copy.start()
        stores.append(copy)

    slots, width = h1.shape
    keys = ck.shape[0]
    half = keys // 2
    tiles = [slice(n, n + 256) for n in range(0, width, 256)]

    def first_norm(rows):
        unit, _ = unit_of(hidden[core, rows].astype(F32))
        h1[rows] = (unit * g1[...] + s1[...]).astype(BF16)

    row_blocks(slots, first_norm)
    scale = HDIM ** (-0.5)
    for n in tiles:
        q[:, n] = ((dot(h1[...], wq[:, n]) + bq[:, n]) * scale).astype(BF16)
        k[:, n] = dot(h1[...], wk[:, n]).astype(BF16)
        v[:, n] = (dot(h1[...], wv[:, n]) + bv[:, n]).astype(BF16)
    store(h1, h1_out)
    store(q, q_out)
    store(k, k_out)
    store(v, v_out)
    key_at = lax.broadcasted_iota(jnp.int32, (slots, slots), 0)
    query_at = lax.broadcasted_iota(jnp.int32, (slots, slots), 1)
    bias[...] = jnp.where((key_at <= query_at) & (key_at < length), 0.0, NEVER)
    nothing = jnp.zeros((HDIM, slots), BF16)

    def attend_pairs(src, key_rows, value_rows, lse, count, other, chunk, adjust):
        lane = lax.broadcasted_iota(jnp.int32, (1, 2 * HDIM), 1) // HDIM

        def pair(p, carry):
            two = pl.ds(pl.multiple_of(p * 2 * HDIM, 2 * HDIM), 2 * HDIM)
            flat_t = src[:, two].T
            spread_heads(qx, p, flat_t, other)
            keys2 = key_rows[:, two]
            values2 = value_rows[:, two]
            tops = []
            for e in range(2):
                top = None
                for c in range(0, count, chunk):
                    s = adjust(keys2[c : c + chunk], lane == e, qx[2 * p + e], c, chunk)
                    scores[e, c : c + chunk] = s
                    best = jnp.max(s, axis=0, keepdims=True)
                    top = best if top is None else jnp.maximum(top, best)
                tops.append(top)
            for e in range(2):
                total, mixed = 0.0, 0.0
                for c in range(0, count, chunk):
                    w = jnp.exp(scores[e, c : c + chunk] - tops[e])
                    total = total + jnp.sum(w, axis=0, keepdims=True)
                    mixed = mixed + dot(values2[c : c + chunk], w.astype(BF16), (0, 0))
                lse[2 * p + e] = tops[e] + jnp.log(total)
                own = mixed[HDIM * e : HDIM * (e + 1)] / total
                mixed_t[pl.ds(pl.multiple_of(p * 2 * HDIM, 2 * HDIM) + e * HDIM, HDIM)] = own.astype(BF16)
            return carry

        lax.fori_loop(0, HEADS // 2, pair, 0)

    attend_pairs(
        q, k, v, lse1, slots, nothing, slots,
        lambda rows, mine, qh, c, n: dot(rows, qh) + bias[...],
    )
    mix[...] = mixed_t[...].T
    store(lse1, lse1_out)
    store(mix, mix_out)
    loads[0].wait()
    for n in tiles:
        x1[:, n] = hidden[core, :, n].astype(F32) + dot(mix[...], wo_v[:, n]) + bo[:, n]
    store(x1, x1_out)

    def second_norm(rows):
        unit, _ = unit_of(x1[rows])
        h2[rows] = (unit * g2[...] + s2[...]).astype(BF16)

    row_blocks(slots, second_norm)
    store(h2, h2_out)
    for i in (5, 1, 2, 3, 4):
        loads[i].wait()
    for n in tiles:
        cq[:, n] = ((dot(h2[...], wcq_v[:, n]) + bcq[:, n]) * scale).astype(BF16)
        for at, states in ((0, near_v), (half, far_v)):
            ck[at : at + half, n] = dot(states[...], wck_v[:, n]).astype(BF16)
            cv[at : at + half, n] = (dot(states[...], wcv_v[:, n]) + bcv[:, n]).astype(BF16)
    store(cq, cq_out)
    store(ck, ck_out)
    store(cv, cv_out)
    row = lax.broadcasted_iota(jnp.int32, (half, 2 * HDIM), 0)
    lane = lax.broadcasted_iota(jnp.int32, (half, 2 * HDIM), 1)
    for at, which in ((0, core), (half, 1 - core)):
        live = (row < frames_half) & (row + which * frames_half < frame_total)
        tail[at : at + half] = jnp.where((lane % HDIM == 0) & ~live, NEVER, 0.0).astype(BF16)
    one = (lax.broadcasted_iota(jnp.int32, (HDIM, slots), 0) == 0).astype(F32).astype(BF16)
    attend_pairs(
        cq, ck, cv, lse2, keys, one, 512,
        lambda rows, mine, qh, c, n: dot(jnp.where(mine, rows, tail[c : c + n]), qh),
    )
    cmix[...] = mixed_t[...].T
    store(lse2, lse2_out)
    store(cmix, cmix_out)
    loads[6].wait()
    for n in tiles:
        x2[:, n] = x1[:, n] + dot(cmix[...], wco_v[:, n]) + bco[:, n]
    store(x2, x2_out)
    for copy in stores:
        copy.wait()


def forward(args, near, far, frames_half):
    slots, width = args["hidden"].shape[1:]
    keys = 2 * near.shape[0]
    low = lambda r: shape(r, width)
    outs = [low(slots)] * 4 + [shape(HEADS, 1, slots, dtype=F32), low(slots)]
    outs += [shape(slots, width, dtype=F32), low(slots), low(slots), low(keys), low(keys)]
    outs += [shape(HEADS, 1, slots, dtype=F32), low(slots), shape(slots, width, dtype=F32)]
    names = ("h1", "q", "k", "v", "lse1", "mix", "x1", "h2", "cq", "ck", "cv", "lse2", "cmix", "x2")
    square = pltpu.VMEM((width, width), BF16)
    state = pltpu.VMEM(near.shape, BF16)
    scratch = [square, state, state, square, square, square, square]
    scratch = [state, state] + [square] * 5
    scratch += [pltpu.VMEM(o.shape, o.dtype) for o in outs]
    scratch += [
        pltpu.VMEM((HEADS, 2 * HDIM, slots), BF16),
        pltpu.VMEM((slots, slots), F32),
        pltpu.VMEM((keys, 2 * HDIM), BF16),
        pltpu.VMEM((width, slots), BF16),
        pltpu.VMEM((2, keys, slots), F32),
        pltpu.SemaphoreType.DMA((7,)),
        pltpu.SemaphoreType.DMA((len(outs),)),
    ]
    a = args
    result = pl.pallas_call(
        functools.partial(forward_kernel, frames_half=frames_half),
        out_shape=outs,
        in_specs=[SMEM, SMEM] + [VMEM] * 14 + [ANY] * 7,
        out_specs=[ANY] * len(outs),
        scratch_shapes=scratch,
        compiler_params=pltpu.CompilerParams(vmem_limit_bytes=52 * MIB),
        cost_estimate=pl.CostEstimate(flops=18 * 10**9, bytes_accessed=30 * 10**6, transcendentals=10**7),
        name="forward",
    )(
        a["lengths"], a["frame_counts"], a["hidden"], a["first_gain"], a["first_shift"],
        a["self_query"], a["self_query_bias"], a["self_key"], a["self_value"], a["self_value_bias"],
        a["self_out_bias"], a["second_gain"], a["second_shift"], a["cross_query_bias"],
        a["cross_value_bias"], a["cross_out_bias"], near, far, a["self_out"], a["cross_query"],
        a["cross_key"], a["cross_value"], a["cross_out"],
    )
    return dict(zip(names, result))


def flip(bit, here):
    return bit + here - 2 * bit * here


def place(chip, target, owner):
    x = flip(target % 2, chip % 2)
    y = flip(target // 2 % 2, chip // 2 % 2)
    z = flip(target // 4 % 2, chip // 4 % 2) + 2 * flip(target // 8, chip // 8)
    return (x * (2 - owner) + y * (1 + owner)) * 4 + z


def feed_kernel(
    lengths,
    corpus,
    weights,
    x2,
    cotangent,
    g3,
    s3,
    we,
    be,
    ws,
    bs,
    out_ref,
    dx2_ref,
    rows_ref,
    expand_out,
    shrink_out,
    h3,
    dm,
    dm_t,
    act,
    dz,
    acc,
    dh3,
    expand_v,
    shrink_v,
    sems,
    *,
    halving,
):
    core = lax.axis_index("frm")
    chip = lax.axis_index("seq")
    step = pl.program_id(0)
    steps = pl.num_programs(0)
    slots, width = h3.shape
    tiles = [slice(n, n + 256) for n in range(0, width, 256)]
    length = lengths[core]
    weight = weights[corpus[core]]

    @pl.when(step == 0)
    def _():
        def start(rows):
            unit, _ = unit_of(x2[rows])
            h3[rows] = (unit * g3[...] + s3[...]).astype(BF16)
            at = lax.broadcasted_iota(jnp.int32, (rows.size, 1), 0) + rows.start
            grad = cotangent[core, rows].astype(F32) * jnp.where(at < length, weight, 0.0)
            dm[rows] = grad.astype(BF16)
            dx2_ref[rows] = grad
            acc[rows] = jnp.zeros_like(grad)
            dh3[rows] = jnp.zeros_like(grad)

        row_blocks(slots, start)
        dm_t[...] = dm[...].T
        rows_ref[...] = jnp.zeros_like(rows_ref)
        rows_ref[6:7] = jnp.sum(dm[...].astype(F32), axis=0, keepdims=True)

    def copies(tile, which):
        if not halving:
            at = pl.ds(pl.multiple_of(tile * width, width), width)
            pairs = [(expand_v, expand_out.at[at]), (shrink_v, shrink_out.at[:, at])]
            return [pltpu.make_async_copy(*pairs[which], sems.at[which])]
        found = []
        quarter, short, wide = width // 4, width // 16, width // 2
        if which == 0:
            for j in range(4):
                for owner in range(2):
                    at = place(chip, tile * 4 + j, owner)
                    src = expand_v.at[quarter * j : quarter * (j + 1), wide * owner : wide * (owner + 1)]
                    found.append((src, expand_out.at[flip(owner, core), at]))
        else:
            owner = tile // 2
            for target in range(16):
                at = place(chip, target, owner)
                for j in range(2):
                    src = shrink_v.at[short * target : short * (target + 1), wide * j : wide * (j + 1)]
                    to = pl.ds(pl.multiple_of((tile % 2 * 2 + j) * short, short), short)
                    found.append((src, shrink_out.at[flip(owner, core), at, to]))
        return [
            pltpu.make_async_copy(src, dst, sems.at[8 * which + i])
            for i, (src, dst) in enumerate(found)
        ]

    for n in tiles:
        z = dot(h3[...], we[:, n]) + be[:, n]
        half = 0.5 * (1.0 + lax.erf(z * (2.0**-0.5)))
        act[:, n] = (z * half).astype(BF16)
        slope = half + z * (jnp.exp(-0.5 * z * z) * ((2.0 * jnp.pi) ** -0.5))
        dact = dot(dm[...], ws[n, :], (1, 1)).astype(BF16).astype(F32)
        low = (dact * slope).astype(BF16)
        dz[:, n] = low
        rows_ref[pl.ds(step, 1), n] = jnp.sum(low.astype(F32), axis=0, keepdims=True)

    @pl.when(step > 0)
    def _():
        for copy in copies(step - 1, 0) + copies(step - 1, 1):
            copy.wait()

    for n in tiles:
        shrink_v[:, n] = dot(dm_t[...], act[:, n]).astype(BF16)
    for copy in copies(step, 1):
        copy.start()
    for n in tiles:
        expand_v[n, :] = dot(dz[:, n], h3[...], (0, 0)).astype(BF16)
    for copy in copies(step, 0):
        copy.start()
    for n in tiles:
        acc[:, n] += dot(act[...], ws[:, n])
        dh3[:, n] += dot(dz[...], we[n, :], (1, 1))

    @pl.when(step == steps - 1)
    def _():
        def finish(rows):
            value = x2[rows]
            out_ref[rows] = (value + acc[rows] + bs[...]).astype(BF16)
            unit, rstd = unit_of(value)
            grad = dh3[rows]
            dx2_ref[rows] += norm_back(grad, unit, rstd, g3[...])
            rows_ref[4:5] += jnp.sum(grad * unit, axis=0, keepdims=True)
            rows_ref[5:6] += jnp.sum(grad, axis=0, keepdims=True)

        row_blocks(slots, finish)
        for copy in copies(step, 0) + copies(step, 1):
            copy.wait()


def feed(a, x2, halving):
    slots, width = x2.shape
    wide = a["expand_weight"].shape[1]
    whole = lambda *dims: pl.BlockSpec(dims, lambda j: (0,) * len(dims))
    if halving:
        grads = [shape(2, 16, width // 4, width // 2)] * 2
    else:
        grads = [shape(wide, width), shape(width, wide)]
    low = pltpu.VMEM((slots, width), BF16)
    full = pltpu.VMEM((slots, width), F32)
    square = pltpu.VMEM((width, width), BF16)
    return pl.pallas_call(
        functools.partial(feed_kernel, halving=halving),
        grid=(wide // width,),
        out_shape=[shape(slots, width), shape(slots, width, dtype=F32), shape(8, width, dtype=F32)] + grads,
        in_specs=[
            SMEM,
            SMEM,
            SMEM,
            whole(slots, width),
            whole(2, slots, width),
            whole(1, width),
            whole(1, width),
            pl.BlockSpec((width, width), lambda j: (0, j)),
            pl.BlockSpec((1, width), lambda j: (0, j)),
            pl.BlockSpec((width, width), lambda j: (j, 0)),
            whole(1, width),
        ],
        out_specs=[whole(slots, width), whole(slots, width), whole(8, width), ANY, ANY],
        scratch_shapes=[
            low, low, pltpu.VMEM((width, slots), BF16), low, low, full, full, square, square,
            pltpu.SemaphoreType.DMA((40,)),
        ],
        compiler_params=pltpu.CompilerParams(vmem_limit_bytes=52 * MIB),
        cost_estimate=pl.CostEstimate(flops=13 * 10**9, bytes_accessed=25 * 10**6, transcendentals=3 * 10**6),
        name="feed",
    )(
        a["lengths"], a["corpus_ids"], a["corpus_weights"], x2, a["cotangent"], a["third_gain"],
        a["third_shift"], a["expand_weight"], a["expand_bias"], a["shrink_weight"], a["shrink_bias"],
    )


class Sum:
    def __init__(self, here, got, plane, line, along, own, total, sends, arrivals):
        self.here = here
        self.got, self.plane, self.line, self.along = got, plane, line, along
        self.own, self.total = own, total
        self.sends, self.arrivals = sends, arrivals

    def copy(self, k, src, dst, to):
        return pltpu.make_async_remote_copy(
            src_ref=src,
            dst_ref=dst,
            send_sem=self.sends.at[k],
            recv_sem=self.arrivals.at[k],
            device_id=to,
            device_id_type=MESH,
        )

    def pair(self, theirs):
        return self.copy(0, theirs, self.got, self.here.peer)

    def first(self):
        return self.copy(1, self.got.at[8:16], self.plane, self.here.first)

    def second(self):
        return self.copy(2, self.got.at[4:8], self.line, self.here.second)

    def third(self):
        return [
            self.copy(3 + k, self.got.at[k + 1], self.along.at[k], self.here.along[k]) for k in range(3)
        ]

    def last(self):
        return [
            self.copy(6, self.own, self.total.at[self.here.core], self.here.peer),
            pltpu.make_async_copy(self.own, self.total.at[self.here.core], self.sends.at[7]),
        ]

    def add(self, count, other):
        def one(i, carry):
            self.got[i] = self.got[i] + other[i]
            return carry

        lax.fori_loop(0, count, one, 0)

    def start(self, theirs):
        self.pair(theirs).start()

    def step_pair(self, theirs, mine):
        self.pair(theirs).wait()
        self.add(16, mine)
        self.first().start()

    def step_first(self):
        self.first().wait()
        self.add(8, self.plane)
        self.second().start()

    def step_second(self):
        self.second().wait()
        self.add(4, self.line)
        for copy in self.third():
            copy.start()

    def step_third(self):
        for copy in self.third():
            copy.wait()
        total = self.got[0].astype(F32)
        for k in range(3):
            total = total + self.along[k].astype(F32)
        self.own[...] = total.astype(BF16)
        for copy in self.last():
            copy.start()

    def step_last(self):
        for copy in self.last():
            copy.wait()


class Here:
    def __init__(self):
        self.core = core = lax.axis_index("frm")
        self.chip = chip = lax.axis_index("seq")
        by_x = 1 - 2 * (chip % 2)
        by_y = 2 - 4 * (chip // 2 % 2)
        by_z = 4 - 8 * (chip // 4 % 2)
        by_zz = 8 - 16 * (chip // 8)
        self.peer = (chip, 1 - core)
        self.x = (chip + by_x, core)
        self.y = (chip + by_y, core)
        self.first = (chip + by_x * (1 - core) + by_y * core, core)
        self.second = (chip + by_y * (1 - core) + by_x * core, core)
        self.along = [(chip + by_z, core), (chip + by_zz, core), (chip + by_z + by_zz, core)]

    def meet(self):
        barrier = pltpu.get_barrier_semaphore()
        others = [self.peer, self.x, self.y] + self.along
        for other in others:
            pl.semaphore_signal(barrier, inc=1, device_id=other, device_id_type=MESH)
        pl.semaphore_wait(barrier, len(others))


BACK_BIG = (
    "dx2", "wco", "cmix", "ck", "cv", "cq", "lse2", "near", "far", "h2", "x1", "wcq", "wck", "wcv",
    "wo", "mix", "q", "k", "v", "lse1", "h1", "hidden", "wq", "wk", "wv", "rows", "out", "expand", "shrink",
)


def backward_kernel(lengths, frames, g1, g2, *refs, frames_half, halving):
    big = dict(zip(BACK_BIG, refs))
    refs = refs[len(BACK_BIG) :]
    (
        sums_expand, sums_shrink, sums_cross, sums_self, gh_out, ge_out, vec_out, out_out,
        dx, w0, w1, w2, w3, cmix, ck, cv, cq, lse, near, far, h2, x1, hidden, dmix, dq_t, k_t, qx, dmx,
        tail, bias, vec, vec_got, vec_sum, grads, mine, low, own, got, plane, line, along,
        in_sem, sends, arrivals, more_sends, more_arrivals,
    ) = refs
    here = Here()
    core, chip = here.core, here.chip
    slots, width = cq.shape
    keys = ck.shape[0]
    half = keys // 2
    length = lengths[core]
    frame_total = frames[core]
    tiles = [slice(n, n + 256) for n in range(0, width, 256)]

    def load(name, dst, src=None):
        i = BACK_BIG.index(name)
        copy = pltpu.make_async_copy(big[name] if src is None else src, dst, in_sem.at[i])
        return copy

    q, k = ck.at[0:slots], ck.at[slots : 2 * slots]
    v, mix, h1 = cv.at[0:slots], cv.at[slots : 2 * slots], cv.at[2 * slots : 3 * slots]
    early = [
        load("dx2", dx), load("wco", w0), load("cmix", cmix), load("ck", ck), load("cv", cv),
        load("cq", cq), load("lse2", lse), load("wcq", w1), load("h2", h2), load("x1", x1),
        load("near", near), load("far", far), load("wck", w2), load("wcv", w3),
        load("hidden", hidden, big["hidden"].at[core]), load("rows", vec.at[0:8]),
    ]
    late = [
        load("wo", w0), load("wq", w1), load("wk", w2), load("wv", w3),
        load("q", q), load("k", k), load("v", v), load("mix", mix), load("h1", h1), load("lse1", lse),
    ]
    early = {name: copy for name, copy in zip(
        ("dx2", "wco", "cmix", "ck", "cv", "cq", "lse2", "wcq", "h2", "x1", "near", "far", "wck", "wcv", "hidden", "rows"),
        early)}
    late = {name: copy for name, copy in zip(
        ("wo", "wq", "wk", "wv", "q", "k", "v", "mix", "h1", "lse1"), late)}
    for copy in early.values():
        copy.start()

    ours, others = core, 1 - core
    if halving:
        here.meet()
        totals = (sums_expand, sums_shrink, sums_cross, sums_self)
        units = [
            Sum(here, got.at[u], plane.at[u], line.at[u], along.at[u], own.at[u], totals[u],
                sends.at[u], arrivals.at[u])
            for u in range(4)
        ]
        feed_mine = [load("expand", mine, big["expand"].at[0]), load("shrink", mine, big["shrink"].at[0])]
        feed_theirs = [big["expand"].at[1], big["shrink"].at[1]]
        units[0].start(feed_theirs[0])
        feed_mine[0].start()
        units[1].start(feed_theirs[1])

        def extra(i, src, dst):
            return pltpu.make_async_remote_copy(
                src_ref=src, dst_ref=dst, send_sem=more_sends.at[i], recv_sem=more_arrivals.at[i],
                device_id=here.peer, device_id_type=MESH,
            )

        def stay(i, src, dst):
            return pltpu.make_async_copy(src, dst, more_sends.at[i])

        out_copies = [extra(0, big["out"], out_out.at[core]), stay(1, big["out"], out_out.at[core])]
        for copy in out_copies:
            copy.start()

    def pair_units(u, theirs, own_part):
        if halving:
            units[u].step_pair(theirs, own_part)

    def event(name):
        if not halving:
            return
        if name == "feed0 pair":
            feed_mine[0].wait()
            units[0].step_pair(feed_theirs[0], mine)
            feed_mine[1].start()
        elif name == "feed1 pair":
            feed_mine[1].wait()
            units[1].step_pair(feed_theirs[1], mine)
        else:
            unit, what = name.split()
            getattr(units[int(unit)], "step_" + what)()

    def column_sum(row, value):
        ones = jnp.ones((16, value.shape[0]), BF16)
        vec[row : row + 1] = dot(ones, value[...])[0:1]

    def put(member, rows, value, away=1):
        low_value = value.astype(BF16)
        if not halving:
            grads[member, rows] = low_value
            return
        short, wide = width // 16, width // 2
        first = rows.start // short
        count = (rows.stop - rows.start) // short
        for i in range(count):
            for owner in range(2):
                at = place(chip, first + i, owner)
                grads[flip(owner, core) * away, at, short * member : short * (member + 1)] = low_value[
                    short * i : short * (i + 1), wide * owner : wide * (owner + 1)
                ]

    wide_tiles = [slice(n, n + 384) for n in range(0, width, 384)]

    def weight_grad(member, left_t, left, right, away=1):
        for n in wide_tiles:
            if left_t is not None:
                value = dot(left_t[n, :], right)
            else:
                value = dot(left[:, n], right, (0, 0))
            put(member, n, value, away)

    def attention_back(src_q, src_k, src_v, src_mix, count, block, scored, other, after):
        lane = lax.broadcasted_iota(jnp.int32, (1, 2 * HDIM), 1)
        nothing = jnp.zeros((HDIM, slots), BF16)

        def pair(p, carry):
            at = pl.multiple_of(p * 2 * HDIM, 2 * HDIM)
            two = pl.ds(at, 2 * HDIM)
            q2 = src_q[:, two]
            dm2 = dmix[:, two]
            dm2_t = dm2.T
            spread_heads(qx, 0, q2.T, other)
            spread_heads(dmx, 0, dm2_t, nothing)
            k_t[:, 0:count] = src_k[:, two].T
            overlap = dm2_t.astype(F32) * src_mix[:, two].T.astype(F32)
            delta = [jnp.sum(overlap[HDIM * e : HDIM * (e + 1)], axis=0, keepdims=True) for e in range(2)]
            for b in range(0, count, block):
                rows = slice(b, b + block)
                keys2, values2 = src_k[rows, two], src_v[rows, two]
                dks, dvs = [], []
                for e in range(2):
                    s = scored(keys2, (lane // HDIM) == e, qx[e], rows)
                    w = jnp.exp(s - lse[2 * p + e])
                    dp = dot(values2, dmx[e])
                    ds = (w * (dp - delta[e])).astype(BF16)
                    dvs.append(dot(w.astype(BF16), dm2))
                    dks.append(dot(ds, q2))
                    dq = dot(k_t[HDIM * e : HDIM * (e + 1), rows], ds)
                    head = pl.ds(at + HDIM * e, HDIM)
                    if b == 0:
                        dq_t[head] = dq
                    else:
                        dq_t[head] += dq
                src_k[rows, two] = jnp.where(lane < HDIM, dks[0], dks[1]).astype(BF16)
                src_v[rows, two] = jnp.where(lane < HDIM, dvs[0], dvs[1]).astype(BF16)
            after(p)
            return carry

        lax.fori_loop(0, HEADS // 2, pair, 0)

    def events_at(table):
        def after(p):
            for number, names in table.items():

                @pl.when(p == number)
                def _(names=names):
                    for name in names:
                        event(name)

        return after

    vec[8:24] = jnp.zeros((16, width), F32)
    for name in ("dx2", "wco", "cmix"):
        early[name].wait()
    low[...] = dx[...].astype(BF16)
    for n in tiles:
        dmix[:, n] = dot(low[...], w0[n, :], (1, 1)).astype(BF16)
    weight_grad(0, None, low, cmix[...])
    column_sum(8, low)
    late["wo"].start()
    row = lax.broadcasted_iota(jnp.int32, (half, 2 * HDIM), 0)
    lane = lax.broadcasted_iota(jnp.int32, (half, 2 * HDIM), 1)
    for at, which in ((0, core), (half, 1 - core)):
        live = (row < frames_half) & (row + which * frames_half < frame_total)
        tail[at : at + half] = jnp.where((lane % HDIM == 0) & ~live, NEVER, 0.0).astype(BF16)
    one = (lax.broadcasted_iota(jnp.int32, (HDIM, slots), 0) == 0).astype(F32).astype(BF16)
    for name in ("ck", "cv", "cq", "lse2"):
        early[name].wait()
    attention_back(
        cq, ck, cv, cmix, keys, 512,
        lambda rows2, mine2, qh, rows: dot(jnp.where(mine2, rows2, tail[rows]), qh),
        one,
        events_at(EVENTS_CROSS),
    )
    low_scale = HDIM ** (-0.5)
    for name in ("wcq", "h2", "x1"):
        early[name].wait()
    column_t = (dq_t[...] * low_scale).astype(BF16)
    low[...] = column_t.T
    weight_grad(1, column_t, None, h2[...])
    column_sum(9, low)

    def norm_step(value, grad_of, gain, gain_row):
        def one_block(rows):
            unit, rstd = unit_of(value(rows))
            grad = grad_of(rows)
            dx[rows] += norm_back(grad, unit, rstd, gain[...])
            vec[gain_row : gain_row + 1] += jnp.sum(grad * unit, axis=0, keepdims=True)
            vec[gain_row + 1 : gain_row + 2] += jnp.sum(grad, axis=0, keepdims=True)

        row_blocks(slots, one_block)

    norm_step(lambda rows: x1[rows], lambda rows: dot(low[rows], w1[...], (1, 1)), g2, 11)
    late["wq"].start()
    for name in ("near", "far", "wck", "wcv"):
        early[name].wait()
    column_sum(10, cv)
    for member, d in ((2, ck), (3, cv)):
        for n in wide_tiles:
            value = dot(d[0:half, n], near[...], (0, 0)) + dot(d[half:keys, n], far[...], (0, 0))
            put(member, n, value)
    if halving:
        units[2].start(grads.at[1])
    event_after_cross = EVENTS_MIDDLE

    def states_back(out):
        def one_block(rows, lead):
            inner = pl.ds(pl.multiple_of(rows.start + lead, rows.size), rows.size)
            out[rows] = (dot(ck[inner], w2[...], (1, 1)) + dot(cv[inner], w3[...], (1, 1))).astype(BF16)

        return one_block

    row_blocks(half, lambda rows: states_back(near)(rows, 0), 256)
    row_blocks(half, lambda rows: states_back(far)(rows, half), 256)
    if halving:
        ge_copies = [extra(2, far, ge_out.at[core]), stay(3, near, ge_out.at[core])]
    else:
        ge_copies = [
            pltpu.make_async_copy(near, ge_out.at[0], more_sends.at[2]),
            pltpu.make_async_copy(far, ge_out.at[1], more_sends.at[3]),
        ]
    for copy in ge_copies:
        copy.start()
    for name in ("wk", "wv", "q", "k", "v", "mix", "h1", "lse1"):
        late[name].start()
    for name in event_after_cross:
        if name == "2 pair":
            if halving:
                units[2].step_pair(grads.at[1], grads.at[0])
        else:
            event(name)
    if not halving:
        spill = pltpu.make_async_copy(grads, sums_cross, more_sends.at[0])
        spill.start()
        spill.wait()
    for name in ("wo", "q", "k", "v", "mix", "h1", "lse1"):
        late[name].wait()
    low[...] = dx[...].astype(BF16)
    for n in tiles:
        dmix[:, n] = dot(low[...], w0[n, :], (1, 1)).astype(BF16)
    weight_grad(0, None, low, mix[...], 2)
    column_sum(13, low)
    key_at = lax.broadcasted_iota(jnp.int32, (slots, slots), 0)
    query_at = lax.broadcasted_iota(jnp.int32, (slots, slots), 1)
    bias[...] = jnp.where((key_at <= query_at) & (key_at < length), 0.0, NEVER)
    attention_back(
        q, k, v, mix, slots, slots,
        lambda rows2, mine2, qh, rows: dot(rows2, qh) + bias[rows],
        nothing_rows(slots),
        events_at(EVENTS_SELF),
    )
    column_t = (dq_t[...] * low_scale).astype(BF16)
    low[...] = column_t.T
    weight_grad(1, column_t, None, h1[...], 2)
    weight_grad(2, None, k, h1[...], 2)
    weight_grad(3, None, v, h1[...], 2)
    if halving:
        units[3].start(grads.at[2])
    column_sum(14, low)
    column_sum(15, v)
    for name in ("wq", "wk", "wv"):
        late[name].wait()
    early["hidden"].wait()

    def dh1(rows):
        return (
            dot(low[rows], w1[...], (1, 1))
            + dot(k[rows], w2[...], (1, 1))
            + dot(v[rows], w3[...], (1, 1))
        )

    early["rows"].wait()
    norm_step(lambda rows: hidden[rows].astype(F32), dh1, g1, 16)
    low[...] = dx[...].astype(BF16)
    if halving:
        gh_copies = [extra(4, low, gh_out.at[core]), stay(5, low, gh_out.at[core])]
    else:
        gh_copies = [
            pltpu.make_async_copy(low, gh_out.at[0], more_sends.at[4]),
            pltpu.make_async_copy(vec, vec_out, more_sends.at[5]),
            pltpu.make_async_copy(grads, sums_self, more_sends.at[6]),
        ]
    for copy in gh_copies:
        copy.start()
    if halving:
        vec_to = [here.peer, here.x, here.y] + here.along[:2]

        def vec_copy(i):
            return pltpu.make_async_remote_copy(
                src_ref=vec_sum.at[i], dst_ref=vec_got.at[i], send_sem=more_sends.at[8 + i],
                recv_sem=more_arrivals.at[8 + i], device_id=vec_to[i], device_id_type=MESH,
            )

        def vec_step(i):
            vec_copy(i).wait()
            vec_sum[i + 1] = vec_sum[i] + vec_got[i]
            if i < 4:
                vec_copy(i + 1).start()

        vec_sum[0] = vec[...]
        vec_copy(0).start()
        for name in EVENTS_TAIL:
            if name == "3 pair":
                units[3].step_pair(grads.at[2], grads.at[0])
            elif name.startswith("vec"):
                vec_step(int(name.split()[1]))
            else:
                event(name)
        spill = pltpu.make_async_copy(vec_sum.at[5], vec_out, more_sends.at[6])
        spill.start()
        spill.wait()
        for copy in out_copies:
            copy.wait()
    for copy in ge_copies + gh_copies:
        copy.wait()


def nothing_rows(slots):
    return jnp.zeros((HDIM, slots), BF16)


EVENTS_CROSS = {
    0: ("feed0 pair",),
    1: ("feed1 pair",),
    4: ("0 first",),
}
EVENTS_MIDDLE = ("1 first", "0 second", "2 pair")
EVENTS_SELF = {3: ("1 second", "0 third")}
EVENTS_TAIL = (
    "3 pair", "vec 0", "2 first", "vec 1", "1 third", "3 first", "vec 2", "2 second", "vec 3",
    "3 second", "vec 4", "2 third", "3 third", "0 last", "1 last", "2 last", "3 last",
)


def backward(a, kept, near, far, out, dx2, rows, expand, shrink, frames_half, halving):
    slots, width = dx2.shape
    big = dict(kept)
    big.update(
        dx2=dx2, near=near, far=far, out=out, expand=expand, shrink=shrink, rows=rows, hidden=a["hidden"],
        wco=a["cross_out"], wcq=a["cross_query"], wck=a["cross_key"], wcv=a["cross_value"],
        wo=a["self_out"], wq=a["self_query"], wk=a["self_key"], wv=a["self_value"],
    )
    part = (width // 4, width // 2)
    if halving:
        outs = [shape(2, *part)] * 4
        outs += [shape(2, slots, width), shape(2, *near.shape), shape(24, width, dtype=F32), shape(2, slots, width)]
        grads = pltpu.VMEM((3, 16) + part, BF16)
        buffers = [
            pltpu.VMEM((16,) + part, BF16),
            pltpu.VMEM((slots, width), BF16),
            pltpu.VMEM((4,) + part, BF16),
            pltpu.VMEM((4, 16) + part, BF16),
            pltpu.VMEM((4, 8) + part, BF16),
            pltpu.VMEM((4, 4) + part, BF16),
            pltpu.VMEM((4, 3) + part, BF16),
        ]
    else:
        outs = [shape(16, 128)] * 2 + [shape(4, width, width)] * 2
        outs += [shape(1, slots, width), shape(2, *near.shape), shape(24, width, dtype=F32), shape(16, 128)]
        grads = pltpu.VMEM((4, width, width), BF16)
        tiny = pltpu.VMEM((16, 128), BF16)
        buffers = [tiny, pltpu.VMEM((slots, width), BF16), tiny, tiny, tiny, tiny, tiny]
    low = pltpu.VMEM((slots, width), BF16)
    square = pltpu.VMEM((width, width), BF16)
    tall = pltpu.VMEM((2 * near.shape[0], width), BF16)
    state = pltpu.VMEM(near.shape, BF16)
    full = pltpu.VMEM((slots, width), F32)
    pair = pltpu.VMEM((2, 2 * HDIM, slots), BF16)
    scratch = [
        full, square, square, square, square, low, tall, tall, low,
        pltpu.VMEM((HEADS, 1, slots), F32), state, state, low, full, low, low,
        pltpu.VMEM((width, slots), F32),
        pltpu.VMEM((2 * HDIM, 2 * near.shape[0]), BF16), pair, pair,
        pltpu.VMEM((2 * near.shape[0], 2 * HDIM), BF16),
        pltpu.VMEM((slots, slots), F32),
        pltpu.VMEM((24, width), F32), pltpu.VMEM((5, 24, width), F32), pltpu.VMEM((6, 24, width), F32),
        grads,
    ] + buffers + [
        pltpu.SemaphoreType.DMA((len(BACK_BIG),)),
        pltpu.SemaphoreType.DMA((4, 8)),
        pltpu.SemaphoreType.DMA((4, 8)),
        pltpu.SemaphoreType.DMA((16,)),
        pltpu.SemaphoreType.DMA((16,)),
    ]
    params = dict(vmem_limit_bytes=62 * MIB)
    if halving:
        params.update(collective_id=0, has_side_effects=True)
    return pl.pallas_call(
        functools.partial(backward_kernel, frames_half=frames_half, halving=halving),
        out_shape=outs,
        in_specs=[SMEM, SMEM, VMEM, VMEM] + [ANY] * len(BACK_BIG),
        out_specs=[ANY] * len(outs),
        scratch_shapes=scratch,
        compiler_params=pltpu.CompilerParams(**params),
        cost_estimate=pl.CostEstimate(flops=40 * 10**9, bytes_accessed=50 * 10**6, transcendentals=10**7),
        name="backward",
    )(a["lengths"], a["frame_counts"], a["first_gain"], a["second_gain"], *[big[n] for n in BACK_BIG])


def finish_kernel(expand, shrink, cross, own, vec, gh, *outs):
    chip = lax.axis_index("seq")
    width = vec.shape[1]
    short, wide = width // 16, width // 2
    matrices = outs[:10]
    vectors = outs[10:24]
    hidden_out = outs[24]
    for owner in range(2):
        at = slice(wide * owner, wide * (owner + 1))
        for m in range(4):
            rows = slice(short * m, short * (m + 1))
            matrices[m][:, at] = own[owner, rows].astype(F32)
            matrices[4 + m][:, at] = cross[owner, rows].astype(F32)
            lead = 2 * width * owner + wide * m
            matrices[9][:, lead : lead + wide] = shrink[owner, rows].astype(F32)
        matrices[8][:, at] = expand[owner].astype(F32)
    turned = pltpu.roll(vec[...], width - short * chip, 1)
    order = (16, 17, 14, 15, 13, 11, 12, 9, 10, 8, 4, 5, 6)
    for i, row in enumerate(order):
        vectors[i][...] = turned[row : row + 1, 0:short]
    quarter = width // 4
    line = pltpu.roll(vec[0:8], width - quarter * (chip % 4), 1)
    mine = chip // 4
    picked = jnp.where(lax.broadcasted_iota(jnp.int32, (8, quarter), 0) == mine, line[:, 0:quarter], 0.0)
    vectors[13][...] = jnp.sum(picked, axis=0, keepdims=True)
    hidden_out[...] = gh[...].astype(F32)


def finish(expand, shrink, cross, own, vec, gh):
    width = vec.shape[1]
    short = width // 16
    outs = [shape(short, width, dtype=F32)] * 8
    outs += [shape(width // 4, width, dtype=F32), shape(short, 4 * width, dtype=F32)]
    outs += [shape(1, short, dtype=F32)] * 13 + [shape(1, width // 4, dtype=F32)]
    outs += [shape(*gh.shape, dtype=F32)]
    return pl.pallas_call(
        finish_kernel,
        out_shape=outs,
        in_specs=[VMEM] * 6,
        out_specs=[VMEM] * len(outs),
        compiler_params=pltpu.CompilerParams(vmem_limit_bytes=40 * MIB),
        name="finish",
    )(expand, shrink, cross, own, vec, gh)


NAMES = (
    "hidden", "encoder", "cotangent", "lengths", "frame_counts", "corpus_ids", "corpus_weights",
    "first_gain", "first_shift", "self_query", "self_query_bias", "self_key", "self_value",
    "self_value_bias", "self_out", "self_out_bias", "second_gain", "second_shift", "cross_query",
    "cross_query_bias", "cross_key", "cross_value", "cross_value_bias", "cross_out",
    "cross_out_bias", "third_gain", "third_shift", "expand_weight", "expand_bias", "shrink_weight",
    "shrink_bias",
)


def swap(value):
    return lax.ppermute(value, "frm", [(0, 1), (1, 0)])


def shards(*values):
    a = dict(zip(NAMES, values))
    core = lax.axis_index("frm")
    halving = lax.axis_size("seq") == 16
    for name, value in a.items():
        if value.ndim == 1 and value.dtype == F32 and name != "corpus_weights":
            a[name] = value.reshape(1, -1)
    local = a["encoder"].shape[1]
    padding = ((0, -local % 256), (0, 0))
    pick = lambda value, index: lax.dynamic_index_in_dim(value, index, 0, keepdims=False)
    near = jnp.pad(pick(a["encoder"], core), padding)
    far = swap(jnp.pad(pick(a["encoder"], 1 - core), padding))
    kept = forward(a, near, far, local)
    x2 = kept.pop("x2")
    out, dx2, rows, expand, shrink = feed(a, x2, halving)
    back = backward(a, kept, near, far, out, dx2, rows, expand, shrink, local, halving)
    if halving:
        expand, shrink, cross, own, gh, ge, vec, output = back
        done = finish(expand, shrink, cross, own, vec, gh)
        matrices, vectors, grad_hidden = done[:10], [v.reshape(-1) for v in done[10:24]], done[24]
        own_m, cross_m, expand_m, shrink_m = matrices[:4], matrices[4:8], matrices[8], matrices[9]
        far_grads = ge
        grad_encoder = far_grads[:, :local].astype(F32)
    else:
        _, _, cross, own, gh, ge, vec, _ = back
        add = lambda g, axis: lax.psum(
            lax.psum_scatter(g, "seq", scatter_dimension=axis, tiled=True).astype(BF16), "frm"
        ).astype(F32)
        cross_m = [add(cross[m].astype(F32), 0) for m in range(4)]
        own_m = [add(own[m].astype(F32), 0) for m in range(4)]
        expand_m, shrink_m = add(expand.astype(F32), 0), add(shrink.astype(F32), 0)
        order = (16, 17, 14, 15, 13, 11, 12, 9, 10, 8, 4, 5, 6)
        vectors = [add(vec[row], 0) for row in order] + [add(vec[0:4].reshape(-1), 0)]
        both = lambda own: jnp.stack(
            [jnp.where(core == 0, own, swap(own)), jnp.where(core == 0, swap(own), own)]
        )
        grad_hidden = both(gh[0]).astype(F32)
        output = both(out)
        came = swap(ge[1])
        grad_encoder = jnp.stack(
            [jnp.where(core == 0, ge[0], came), jnp.where(core == 0, came, ge[0])]
        )[:, :local].astype(F32)
    so, sq, sk, sv = [m.T for m in own_m]
    co, cq, ck, cv = [m.T for m in cross_m]
    vg = vectors
    return (
        output, grad_hidden, grad_encoder, vg[0], vg[1], sq, vg[2], sk, sv, vg[3], so, vg[4], vg[5],
        vg[6], cq, vg[7], ck, cv, vg[8], co, vg[9], vg[10], vg[11], expand_m.T, vg[13], shrink_m.T, vg[12],
    )


def solution(mesh):
    return jax.shard_map(
        shards,
        mesh=mesh,
        in_specs=(
            P("seq", None, None),
            P("seq", "frm", None),
            P("seq", None, None),
            P("seq"),
            P("seq"),
            P("seq"),
        )
        + (P(),) * 25,
        out_specs=(P("seq", None, None), P("seq", None, None), P("seq", "frm", None))
        + tuple(
            P(None, "seq") if matrix else P("seq")
            for matrix in (0, 0, 1, 0, 1, 1, 0, 1, 0, 0, 0, 1, 0, 1, 1, 0, 1, 0, 0, 0, 1, 0, 1, 0)
        ),
        check_vma=False,
    )
```
